32 devices in a mesh: groups: 2 (over y), ep: 16 (over z, x, core), tp: 1.
Axes of the slice: x: 2, y: 2, z: 4, core: 2. Of those that a mesh axis runs over, the one named last changes fastest.
Arguments:
- latent: bfloat16 [2, 512, 1024], P(None, ('groups', 'ep'), 'tp'), parts along dimension 1, may hold values from -6 to 6
- routes: int32 [2, 512, 8], P(None, ('groups', 'ep')), parts along dimension 1, may hold values from 0 to 15, all different within a row; in each aligned block of 16 rows (0 to 15, 16 to 31, ..., all dimensions but the last counted through in order) at most 12 rows name the same one
- combine_weights: float32 [2, 512, 8], P(None, ('groups', 'ep')), parts along dimension 1, may hold values from 0.1 to 1
- keep: int32 [16], replicated, may hold values from 6 to 12
- w_gate: bfloat16 [16, 1024, 1024], P('ep', None, 'tp'), may hold values from -0.1875 to 0.1875
- w_up: bfloat16 [16, 1024, 1024], P('ep', None, 'tp'), may hold values from -0.1875 to 0.1875
- w_down: bfloat16 [16, 1024, 1024], P('ep', 'tp'), may hold values from -0.1875 to 0.1875
Outputs:
- mixed: bfloat16 [2, 512, 1024], P(None, ('groups', 'ep'), 'tp'), parts along dimension 1
The draws below stay inside these ranges and needn't reach their ends.
There are 2 independent parts, one for each index of `groups`. The reference program is written for one: setup_inputs(seed, part) draws one part's arguments, and reference() takes and returns one part's arrays. A program takes and returns all parts, laid end to end along the dimension named above; an argument that names none is the same for every part. Nothing has to cross between parts.
Inputs may be any that keep to these rules, and one draw needn't show every extreme that they name: `routes`: in each aligned block of 16 rows of one step, the rows of one index of ep, no expert is named by more than 12 rows; a row names 8 different experts.
All inputs are finite; a program needn't handle non-finite values.
Results may differ from the reference program's by a relative error of at most 0.0065.
Values may be sent and summed in bfloat16 or wider, within the bound.
A program may use at most 64 MiB of HBM per device.

```python
import math
import jax
import jax.numpy as jnp
import numpy as np
from jax import lax

L = 1024
HID = 1024
TOP = 8
STEPS = 2
ROWS_DEV = 16
EXPERTS = 16
CAP = 12
ROWS = 256
N_TP = 1


def draw_keep(key, part):
    key = jax.random.fold_in(key, 11)
    lowest = max(1, CAP // 2)
    values = jax.random.randint(jax.random.fold_in(key, 1), (EXPERTS,), lowest, CAP + 1).astype(jnp.int32)
    order = jax.random.permutation(jax.random.fold_in(key, 2), EXPERTS)
    values = values.at[order[0]].set(CAP).at[order[1]].set(lowest)
    return values.astype(jnp.int32)


def block_scale(rng, shape, cuts, least, largest):
    factor_of, own = 1.0, jax.random.fold_in(rng, 6)
    for position, shards_of in cuts:
        draws = jnp.exp(jax.random.uniform(jax.random.fold_in(own, position), (shards_of,), jnp.float32, least / len(cuts), largest / len(cuts)))
        factor_of = factor_of * jnp.repeat(draws, shape[position] // shards_of).reshape([-1 if axis == position else 1 for axis in range(len(shape))])
    return factor_of


def shared_out(own_key, own, number, rows, number_of, top, reach, lean):
    order = jax.random.permutation(own_key, number_of)
    crowded, usual = load_shares(number_of, rows * top, reach, lean, True), load_shares(number_of, rows * top, reach, lean, False)
    places = jnp.arange(number_of)

    def named(lengths, rotation):
        used = int((lengths > 0).sum())
        fixed = max(1, used // 4)
        moved = fixed + (places - fixed + rotation * (used - fixed)) % max(1, number_of - fixed)
        return jnp.zeros((number_of,), jnp.int32).at[order[jnp.where(places < fixed, places, moved)]].set(jnp.asarray(lengths, jnp.int32))

    lengths = jnp.where(number % 4 == 0, named(crowded, number // 4), named(usual, number - number // 4 - 1))
    mixed = jax.random.permutation(jax.random.fold_in(own, 3), number_of)
    donor, receiver = mixed[0:number_of // 2 * 2:2], mixed[1:number_of // 2 * 2:2]
    slack = jnp.minimum(lengths[donor] - 1, reach - lengths[receiver]) // 2
    slack = jnp.where((donor == order[0]) | (receiver == order[0]) | (lengths[receiver] == 0), 0, jnp.maximum(slack, 0))
    moved = jax.random.randint(jax.random.fold_in(own, 4), (number_of // 2,), 0, 1 << 20) % (slack + 1)
    lengths = lengths.at[donor].add(-moved).at[receiver].add(moved)
    labels = jnp.searchsorted(jnp.cumsum(lengths), jnp.arange(rows * top), side="right").astype(jnp.int32)
    table = labels.reshape(top, rows).T
    table = table[jax.random.permutation(jax.random.fold_in(own, 1), rows)]
    rotation = jax.random.randint(jax.random.fold_in(own, 2), (rows, 1), 0, top)
    return jnp.take_along_axis(table, (jnp.arange(top)[None, :] + rotation) % top, axis=1)


def load_shares(count, total, limit, lean, full):
    portions = [(1 << 20) // math.isqrt(grade ** lean) + 1 for grade in range(1, count + 1)]
    largest = limit if full else min(limit, max(-(-total // count), total * portions[0] // sum(portions)))
    least = 1 if total - largest >= count - 1 else 0
    counts, rest = [largest] + [least] * (count - 1), total - largest - least * (count - 1)
    while rest > 0:
        free = [i for i in range(1, count) if counts[i] < largest] or [i for i in range(1, count) if counts[i] < limit]
        mass, left = sum([portions[i] for i in free]), rest
        for i in free:
            addition = min(limit - counts[i], max(1, left * portions[i] // mass), rest)
            counts[i] = counts[i] + addition
            rest = rest - addition
    return np.array(counts)


def noise(rng, shape, spread, reach, cuts=(), kind=jnp.bfloat16):
    level = block_scale(rng, shape, cuts, -0.22, 0.18) if cuts else 1.0
    result = jax.random.normal(rng, shape, jnp.float32) * spread * level
    return jnp.minimum(jnp.maximum(result, -reach), reach).astype(kind)


def setup_inputs(seed: int = 0, part: int = 0) -> dict:
    seeds = jax.random.split(jax.random.key(seed), 8)
    own_keys = jax.random.split(jax.random.fold_in(seeds[7], part), 8)
    latent = noise(own_keys[0], (STEPS, ROWS, L), 1.0, 6.0, ((1, 16),))
    routes_keys = jax.random.split(jax.random.fold_in(own_keys[1], 1), STEPS * ROWS // ROWS_DEV)
    routes_turns = jax.random.permutation(jax.random.fold_in(own_keys[1], 3), STEPS * ROWS // ROWS_DEV)
    routes = jax.vmap(lambda own, number: shared_out(jax.random.fold_in(own_keys[1], 2), own, number, ROWS_DEV, EXPERTS, TOP, CAP, 2))(routes_keys, routes_turns).reshape((STEPS, ROWS, TOP))
    combine_weights = jnp.clip(0.1 + 0.9 * jax.random.uniform(own_keys[2], (STEPS, ROWS, TOP), jnp.float32) ** block_scale(own_keys[2], (STEPS, ROWS, TOP), ((1, 16),), -0.2, 0.2), 0.1, 1.0)
    keep = draw_keep(jax.random.fold_in(seeds[7], 71), part)
    w_gate = noise(seeds[4], (EXPERTS, L, HID), L ** -0.5, 0.1875, ((0, 16),))
    w_up = noise(seeds[5], (EXPERTS, L, HID), L ** -0.5, 0.1875, ((0, 16),))
    w_down = noise(seeds[6], (EXPERTS, HID, L), HID ** -0.5, 0.1875, ((0, 16),))
    return dict(latent=latent, routes=routes, combine_weights=combine_weights, keep=keep, w_gate=w_gate, w_up=w_up, w_down=w_down)


def expert_apply(rows, gate_w, up_w, down_w):
    gate = jnp.dot(rows, gate_w, preferred_element_type=jnp.float32)
    up = jnp.dot(rows, up_w, preferred_element_type=jnp.float32)
    hidden = (jax.nn.silu(gate) * up).astype(jnp.bfloat16)
    group = down_w.shape[0] // N_TP
    total = jnp.zeros((rows.shape[0], down_w.shape[1]), jnp.float32)
    for piece_index in range(N_TP):
        lower = piece_index * group
        part = jnp.dot(hidden[:, lower:lower + group], down_w[lower:lower + group], preferred_element_type=jnp.float32)
        total = total + part.astype(jnp.bfloat16).astype(jnp.float32)
    return total.astype(jnp.bfloat16)


def reference(latent, routes, combine_weights, keep, w_gate, w_up, w_down):
    nsteps, rows, top = routes.shape
    width = latent.shape[2]
    blocks = rows // ROWS_DEV
    grouped = routes.reshape(nsteps, blocks, ROWS_DEV, top)
    onehot = (grouped[..., None] == jnp.arange(EXPERTS, dtype=jnp.int32)).astype(jnp.int32)
    per_row = jnp.sum(onehot, axis=3)
    before = jnp.cumsum(per_row, axis=2) - per_row
    rank = jnp.take_along_axis(before, grouped, axis=3).astype(jnp.int32)
    kept = rank < keep[grouped]
    slots_each = nsteps * blocks * CAP
    step_ids = jnp.arange(nsteps, dtype=jnp.int32)[:, None, None, None]
    block_ids = jnp.arange(blocks, dtype=jnp.int32)[None, :, None, None]
    row_in = jnp.arange(ROWS_DEV, dtype=jnp.int32)[None, None, :, None]
    row_ids = jnp.broadcast_to(step_ids * rows + block_ids * ROWS_DEV + row_in, grouped.shape).astype(jnp.int32)
    dropped = EXPERTS * slots_each
    target = jnp.where(kept, grouped * slots_each + step_ids * (blocks * CAP) + block_ids * CAP + rank, dropped).astype(jnp.int32)
    table = jnp.full((dropped + 1,), nsteps * rows, jnp.int32).at[target.reshape(-1)].set(row_ids.reshape(-1))
    table = table[:dropped].reshape(EXPERTS, slots_each)
    flat_rows = jnp.concatenate([latent.reshape(nsteps * rows, width), jnp.zeros((1, width), latent.dtype)], axis=0)

    def one_expert(items):
        return expert_apply(flat_rows[items[0]], items[1], items[2], items[3])

    outputs = lax.map(one_expert, (table, w_gate, w_up, w_down))
    flat_out = jnp.concatenate([outputs.reshape(dropped, width), jnp.zeros((1, width), outputs.dtype)], axis=0)
    picked = flat_out[target]
    weights = combine_weights.reshape(nsteps, blocks, ROWS_DEV, top)
    mixed = jnp.sum(picked.astype(jnp.float32) * weights[..., None], axis=3)
    return mixed.reshape(nsteps, rows, width).astype(jnp.bfloat16)
```

```python
import jax
import jax.numpy as jnp
from jax import lax
from jax.experimental import pallas as pl
from jax.experimental.pallas import tpu as pltpu
from jax.sharding import PartitionSpec as P

ROWS = 16
LANES = 128
MESH = pl.DeviceIdType.MESH


def shards(latent, routes, combine_weights, keep, w_gate, w_up, w_down):
    nsteps, rows_dev, top = routes.shape
    experts = keep.shape[0]
    capacity = min(rows_dev, max(2, 3 * rows_dev * top // (2 * experts)))
    onehot = (routes[..., None] == jnp.arange(experts, dtype=jnp.int32)).astype(jnp.int32)
    per_row = jnp.sum(onehot, axis=2)
    before = jnp.cumsum(per_row, axis=1) - per_row
    rank = jnp.take_along_axis(before, routes, axis=2)
    limits = jnp.sum(onehot * keep, axis=3)
    kept = rank < limits
    dropped = experts * capacity
    slot_index = jnp.where(kept, routes * capacity + rank, dropped)
    source = lax.all_gather(latent, "tp", axis=2, tiled=True)
    send_width = source.shape[2]

    def pack(rows_step, slots_step):
        spread = jnp.broadcast_to(rows_step[:, None, :], (rows_dev, top, send_width)).reshape(
            rows_dev * top, send_width
        )
        buffer = (
            jnp.zeros((dropped + 1, send_width), rows_step.dtype)
            .at[slots_step.reshape(-1)]
            .set(spread)
        )
        return buffer[:dropped].reshape(experts, capacity, send_width)

    def serve(received):
        gate = jnp.einsum("sil,lh->sih", received, w_gate[0], preferred_element_type=jnp.float32)
        up = jnp.einsum("sil,lh->sih", received, w_up[0], preferred_element_type=jnp.float32)
        hidden = (jax.nn.silu(gate) * up).astype(jnp.bfloat16)
        partial_out = jnp.einsum(
            "sih,hl->sil", hidden, w_down[0], preferred_element_type=jnp.float32
        )
        summed = lax.psum_scatter(
            partial_out.astype(jnp.bfloat16), "tp", scatter_dimension=2, tiled=True
        )
        return lax.all_to_all(summed, "ep", split_axis=0, concat_axis=0, tiled=True)

    def deliver(buffer):
        return serve(lax.all_to_all(buffer, "ep", split_axis=0, concat_axis=0, tiled=True))

    buffers = [pack(source[step], slot_index[step]) for step in range(nsteps)]
    returned = [deliver(buffer) for buffer in buffers]
    outputs = []
    for step in range(nsteps):
        back = returned[step]
        half_width = back.shape[2]
        flat_back = jnp.concatenate(
            [back.reshape(dropped, half_width), jnp.zeros((1, half_width), back.dtype)], axis=0
        )
        picked = flat_back[slot_index[step]]
        total = jnp.sum(picked.astype(jnp.float32) * combine_weights[step][..., None], axis=1)
        outputs.append(total.astype(jnp.bfloat16))
    return jnp.stack(outputs, axis=0)


def fused_kernel(
    latent, routes, weights, keep, w_gate, w_up, w_down, out,
    rows, gate_w, up_w, down_w, hidden, part, got_core, sum_core, got_x, sum_x, got_z,
    load_sem, gz_send, gz_recv, gx_send, gx_recv, gc_send, gc_recv,
    rc_send, rc_recv, rx_send, rx_recv, rz_send, rz_recv,
):
    nsteps, _, top = routes.shape
    width = latent.shape[2]
    me = lax.axis_index("ep")
    z, x, c = me // 4, (me // 2) % 2, me % 2
    zs = (z, z + 1 - 2 * (z % 2), (z + 2) % 4, 3 - z)

    def index(zz, xx, cc):
        return zz * 4 + xx * 2 + cc

    def slot(s, owner):
        return rows.at[s, pl.ds(pl.multiple_of(owner * ROWS, ROWS), ROWS)]

    def remote(src, dst, send, recv, device):
        return pltpu.make_async_remote_copy(
            src_ref=src, dst_ref=dst, send_sem=send, recv_sem=recv,
            device_id={"ep": device}, device_id_type=MESH,
        )

    partner_x, partner_c = index(z, 1 - x, c), index(z, x, 1 - c)
    mine = pl.ds(pl.multiple_of(me * ROWS, ROWS), ROWS)
    loads = [
        pltpu.make_async_copy(latent.at[s], rows.at[s, mine, pl.ds(0, width)], load_sem.at[s])
        for s in range(nsteps)
    ]
    for n, (src, dst) in enumerate(((w_gate, gate_w), (w_up, up_w), (w_down, down_w))):
        loads.append(pltpu.make_async_copy(src.at[0], dst, load_sem.at[nsteps + n]))
    for load in loads:
        load.start()

    barrier = pltpu.get_barrier_semaphore()
    peers = [index(zs[1], x, c), index(zs[2], x, c), index(zs[3], x, c), partner_x, partner_c]
    for peer in peers:
        pl.semaphore_signal(barrier, inc=1, device_id={"ep": peer}, device_id_type=MESH)

    experts = keep.shape[0]
    lane = lax.broadcasted_iota(jnp.int32, (ROWS, LANES), 1)
    expert = lane % experts
    piece = lane // experts
    limit = jnp.zeros((ROWS, LANES), jnp.float32)
    for e in range(experts):
        limit = jnp.where(expert == e, keep[e].astype(jnp.float32), limit)
    below = (
        lax.broadcasted_iota(jnp.int32, (ROWS, ROWS), 1)
        < lax.broadcasted_iota(jnp.int32, (ROWS, ROWS), 0)
    ).astype(jnp.float32)
    for s in range(nsteps):
        names, scale = routes[s], weights[s]
        count = jnp.zeros((ROWS, LANES), jnp.float32)
        coef = jnp.zeros((ROWS, LANES), jnp.float32)
        for k in range(top):
            hit = names[:, k:k + 1] == expert
            count = count + jnp.where(hit, 1.0, 0.0)
            coef = coef + jnp.where(hit, scale[:, k:k + 1], 0.0)
        rank = jnp.dot(below, count, preferred_element_type=jnp.float32)
        coef = jnp.where(rank < limit, coef, 0.0)
        first = coef.astype(jnp.bfloat16).astype(jnp.float32)
        second = (coef - first).astype(jnp.bfloat16).astype(jnp.float32)
        third = coef - first - second
        pieces = jnp.where(
            piece == 0, first, jnp.where(piece == 1, second, jnp.where(piece == 2, third, 0.0))
        )
        rows[s, mine, pl.ds(width, LANES)] = pieces.astype(jnp.bfloat16)

    pl.semaphore_wait(barrier, len(peers))

    sends = []

    def start(copy):
        copy.start()
        sends.append(copy)

    def gather_z(s, d):
        return remote(slot(s, me), slot(s, me), gz_send.at[s, d - 1], gz_recv.at[s, d - 1],
                      index(zs[d], x, c))

    def gather_x(s, d):
        ref = slot(s, index(zs[d], x, c))
        return remote(ref, ref, gx_send.at[s, d], gx_recv.at[s, d], partner_x)

    def gather_c(s, d, far):
        ref = slot(s, index(zs[d], (1 - x) if far else x, c))
        return remote(ref, ref, gc_send.at[s, d, far], gc_recv.at[s, d, far], partner_c)

    def wait_z(s, d):
        ref = slot(s, index(zs[d], x, c))
        remote(ref, ref, gz_send.at[s, d - 1], gz_recv.at[s, d - 1], index(zs[d], x, c)).wait_recv()

    def wait_x(s, d):
        ref = slot(s, index(zs[d], 1 - x, c))
        remote(ref, ref, gx_send.at[s, d], gx_recv.at[s, d], partner_x).wait_recv()

    def wait_c(s, d, far):
        ref = slot(s, index(zs[d], (1 - x) if far else x, 1 - c))
        remote(ref, ref, gc_send.at[s, d, far], gc_recv.at[s, d, far], partner_c).wait_recv()

    def gather_own(s):
        loads[s].wait()
        start(gather_x(s, 0))
        for d in (2, 3, 1):
            start(gather_z(s, d))
        start(gather_c(s, 0, 0))

    def gather_forward_z(s):
        for d in (1, 2, 3):
            wait_z(s, d)
            start(gather_x(s, d))
            start(gather_c(s, d, 0))

    def gather_forward_x(s):
        for d in range(4):
            wait_x(s, d)
            start(gather_c(s, d, 1))

    def gather_end(s):
        for far in range(2):
            for d in range(4):
                wait_c(s, d, far)

    tile = 256

    def compute(s, first):
        if first:
            loads[nsteps].wait()
            loads[nsteps + 1].wait()
        for j in range(0, gate_w.shape[1], tile):
            inputs = rows[s, :, pl.ds(0, width)]
            gate = jnp.dot(inputs, gate_w[:, j:j + tile], preferred_element_type=jnp.float32)
            up = jnp.dot(inputs, up_w[:, j:j + tile], preferred_element_type=jnp.float32)
            hidden[:, j:j + tile] = (gate / (1.0 + jnp.exp(-gate)) * up).astype(jnp.bfloat16)
        if first:
            loads[nsteps + 2].wait()
        pick_row = lax.broadcasted_iota(jnp.int32, (LANES, tile), 0)
        pick = jnp.where((pick_row % experts == me) & (pick_row < 3 * experts), 1.0, 0.0)
        coef = jnp.dot(
            rows[s, :, pl.ds(width, LANES)], pick.astype(jnp.bfloat16),
            preferred_element_type=jnp.float32,
        )
        for j in range(0, width, tile):
            result = jnp.dot(hidden[...], down_w[:, j:j + tile], preferred_element_type=jnp.float32)
            result = result.astype(jnp.bfloat16).astype(jnp.float32) * coef
            part[s, :, :, :, :, j:j + tile] = result.astype(jnp.bfloat16).reshape(4, 2, 2, ROWS, tile)

    def reduce_c(s):
        return remote(part.at[s, :, :, 1 - c], got_core.at[s], rc_send.at[s], rc_recv.at[s], partner_c)

    def reduce_x(s):
        return remote(sum_core.at[s, :, 1 - x], got_x.at[s], rx_send.at[s], rx_recv.at[s], partner_x)

    def reduce_z(s, d):
        return remote(sum_x.at[s, d - 1], got_z.at[s, d - 1], rz_send.at[s, d - 1], rz_recv.at[s, d - 1],
                      index(zs[d], x, c))

    def reduce_after_c(s):
        reduce_c(s).wait_recv()
        for zz in range(4):
            for xx in range(2):
                total = part[s, zz, xx, c].astype(jnp.float32) + got_core[s, zz, xx].astype(jnp.float32)
                sum_core[s, zz, xx] = total.astype(jnp.bfloat16)
        start(reduce_x(s))

    def reduce_after_x(s):
        reduce_x(s).wait_recv()
        for d in (2, 3, 1):
            total = sum_core[s, zs[d], x].astype(jnp.float32) + got_x[s, zs[d]].astype(jnp.float32)
            sum_x[s, d - 1] = total.astype(jnp.bfloat16)
            start(reduce_z(s, d))

    def reduce_end(s):
        total = sum_core[s, z, x].astype(jnp.float32) + got_x[s, z].astype(jnp.float32)
        for d in (1, 2, 3):
            reduce_z(s, d).wait_recv()
            total = total + got_z[s, d - 1].astype(jnp.float32)
        out[s] = total.astype(jnp.bfloat16)

    gather_own(0)
    gather_own(1)
    gather_forward_z(0)
    gather_forward_x(0)
    gather_forward_z(1)
    gather_end(0)
    compute(0, True)
    start(reduce_c(0))
    gather_forward_x(1)
    gather_end(1)
    reduce_after_c(0)
    compute(1, False)
    start(reduce_c(1))
    reduce_after_x(0)
    reduce_after_c(1)
    reduce_end(0)
    reduce_after_x(1)
    reduce_end(1)
    for copy in sends:
        copy.wait_send()


def fused(latent, routes, combine_weights, keep, w_gate, w_up, w_down):
    nsteps, nrows, width = latent.shape
    units = w_gate.shape[2]
    blocks = 16 * nrows
    bf16 = jnp.bfloat16
    dma = pltpu.SemaphoreType.DMA
    vmem = pl.BlockSpec(memory_space=pltpu.VMEM)
    hbm = pl.BlockSpec(memory_space=pl.ANY)
    return pl.pallas_call(
        fused_kernel,
        out_shape=jax.ShapeDtypeStruct(latent.shape, bf16),
        in_specs=[hbm, vmem, vmem, pl.BlockSpec(memory_space=pltpu.SMEM), hbm, hbm, hbm],
        out_specs=vmem,
        scratch_shapes=[
            pltpu.VMEM((nsteps, blocks, width + LANES), bf16),
            pltpu.VMEM((width, units), bf16),
            pltpu.VMEM((width, units), bf16),
            pltpu.VMEM((units, width), bf16),
            pltpu.VMEM((blocks, units), bf16),
            pltpu.VMEM((nsteps, 4, 2, 2, nrows, width), bf16),
            pltpu.VMEM((nsteps, 4, 2, nrows, width), bf16),
            pltpu.VMEM((nsteps, 4, 2, nrows, width), bf16),
            pltpu.VMEM((nsteps, 4, nrows, width), bf16),
            pltpu.VMEM((nsteps, 3, nrows, width), bf16),
            pltpu.VMEM((nsteps, 3, nrows, width), bf16),
            dma((nsteps + 3,)),
            dma((nsteps, 3)), dma((nsteps, 3)),
            dma((nsteps, 4)), dma((nsteps, 4)),
            dma((nsteps, 4, 2)), dma((nsteps, 4, 2)),
            dma((nsteps,)), dma((nsteps,)),
            dma((nsteps,)), dma((nsteps,)),
            dma((nsteps, 3)), dma((nsteps, 3)),
        ],
        compiler_params=pltpu.CompilerParams(
            collective_id=0, has_side_effects=True, vmem_limit_bytes=40 * 1024 * 1024
        ),
        cost_estimate=pl.CostEstimate(
            flops=6 * nsteps * blocks * width * units,
            bytes_accessed=6 * width * units,
            transcendentals=nsteps * blocks * units,
        ),
    )(latent, routes, combine_weights, keep, w_gate, w_up, w_down)


def solution(mesh):
    one_group = mesh.shape["ep"] == 16 and mesh.shape["tp"] == 1
    placed = (
        P(None, ("groups", "ep"), "tp"),
        P(None, ("groups", "ep"), None),
        P(None, ("groups", "ep"), None),
        P(),
        P("ep", None, "tp"),
        P("ep", None, "tp"),
        P("ep", "tp", None),
    )
    return jax.shard_map(
        fused if one_group else shards,
        mesh=mesh,
        in_specs=placed,
        out_specs=P(None, ("groups", "ep"), "tp"),
        check_vma=False,
    )
```

```python
import jax
import jax.numpy as jnp
from jax import lax
from jax.experimental import pallas as pl
from jax.experimental.pallas import tpu as pltpu
from jax.sharding import PartitionSpec as P

ROWS = 16
LANES = 128
MESH = pl.DeviceIdType.MESH


def shards(latent, routes, combine_weights, keep, w_gate, w_up, w_down):
    nsteps, rows_dev, top = routes.shape
    experts = keep.shape[0]
    capacity = min(rows_dev, max(2, 3 * rows_dev * top // (2 * experts)))
    onehot = (routes[..., None] == jnp.arange(experts, dtype=jnp.int32)).astype(jnp.int32)
    per_row = jnp.sum(onehot, axis=2)
    before = jnp.cumsum(per_row, axis=1) - per_row
    rank = jnp.take_along_axis(before, routes, axis=2)
    limits = jnp.sum(onehot * keep, axis=3)
    kept = rank < limits
    dropped = experts * capacity
    slot_index = jnp.where(kept, routes * capacity + rank, dropped)
    source = lax.all_gather(latent, "tp", axis=2, tiled=True)
    send_width = source.shape[2]

    def pack(rows_step, slots_step):
        spread = jnp.broadcast_to(rows_step[:, None, :], (rows_dev, top, send_width)).reshape(
            rows_dev * top, send_width
        )
        buffer = (
            jnp.zeros((dropped + 1, send_width), rows_step.dtype)
            .at[slots_step.reshape(-1)]
            .set(spread)
        )
        return buffer[:dropped].reshape(experts, capacity, send_width)

    def serve(received):
        gate = jnp.einsum("sil,lh->sih", received, w_gate[0], preferred_element_type=jnp.float32)
        up = jnp.einsum("sil,lh->sih", received, w_up[0], preferred_element_type=jnp.float32)
        hidden = (jax.nn.silu(gate) * up).astype(jnp.bfloat16)
        partial_out = jnp.einsum(
            "sih,hl->sil", hidden, w_down[0], preferred_element_type=jnp.float32
        )
        summed = lax.psum_scatter(
            partial_out.astype(jnp.bfloat16), "tp", scatter_dimension=2, tiled=True
        )
        return lax.all_to_all(summed, "ep", split_axis=0, concat_axis=0, tiled=True)

    def deliver(buffer):
        return serve(lax.all_to_all(buffer, "ep", split_axis=0, concat_axis=0, tiled=True))

    buffers = [pack(source[step], slot_index[step]) for step in range(nsteps)]
    returned = [deliver(buffer) for buffer in buffers]
    outputs = []
    for step in range(nsteps):
        back = returned[step]
        half_width = back.shape[2]
        flat_back = jnp.concatenate(
            [back.reshape(dropped, half_width), jnp.zeros((1, half_width), back.dtype)], axis=0
        )
        picked = flat_back[slot_index[step]]
        total = jnp.sum(picked.astype(jnp.float32) * combine_weights[step][..., None], axis=1)
        outputs.append(total.astype(jnp.bfloat16))
    return jnp.stack(outputs, axis=0)


def fused_kernel(
    latent, routes, weights, keep, w_gate, w_up, w_down, out,
    rows_first, rows_next, gate_w, up_w, down_w, hidden, part, got_core, sum_core, got_x, sum_x, got_z,
    load_sem, gz_send, gz_recv, gx_send, gx_recv, gc_send, gc_recv,
    rc_send, rc_recv, rx_send, rx_recv, rz_send, rz_recv,
):
    nsteps, top, _ = routes.shape
    width = latent.shape[2]
    me = lax.axis_index("ep")
    z, x, c = me // 4, (me // 2) % 2, me % 2
    zs = (z, z + 1 - 2 * (z % 2), (z + 2) % 4, 3 - z)

    def index(zz, xx, cc):
        return zz * 4 + xx * 2 + cc

    rows = (rows_first, *(rows_next.at[s] for s in range(nsteps - 1)))

    def slot(s, owner):
        return rows[s].at[pl.ds(pl.multiple_of(owner * ROWS, ROWS), ROWS)]

    def remote(src, dst, send, recv, device):
        return pltpu.make_async_remote_copy(
            src_ref=src, dst_ref=dst, send_sem=send, recv_sem=recv,
            device_id={"ep": device}, device_id_type=MESH,
        )

    partner_x, partner_c = index(z, 1 - x, c), index(z, x, 1 - c)
    mine = pl.ds(pl.multiple_of(me * ROWS, ROWS), ROWS)
    loads = [
        pltpu.make_async_copy(latent.at[s], rows[s].at[mine, pl.ds(0, width)], load_sem.at[s])
        for s in range(nsteps)
    ]
    for n, (src, dst) in enumerate(((w_gate, gate_w), (w_up, up_w), (w_down, down_w))):
        loads.append(pltpu.make_async_copy(src.at[0], dst, load_sem.at[nsteps + n]))
    for load in loads:
        load.start()

    barrier = pltpu.get_barrier_semaphore()
    peers = [index(zs[1], x, c), index(zs[2], x, c), index(zs[3], x, c), partner_x, partner_c]
    for peer in peers:
        pl.semaphore_signal(barrier, inc=1, device_id={"ep": peer}, device_id_type=MESH)

    experts = keep.shape[0]
    line = lax.broadcasted_iota(jnp.int32, (LANES, ROWS), 0)
    expert = line % experts
    piece = line // experts
    limit = jnp.zeros((LANES, ROWS), jnp.float32)
    for e in range(experts):
        limit = jnp.where(expert == e, keep[e].astype(jnp.float32), limit)
    row_a = lax.broadcasted_iota(jnp.int32, (ROWS, ROWS), 0)
    row_b = lax.broadcasted_iota(jnp.int32, (ROWS, ROWS), 1)
    before = jnp.where(row_a < row_b, 1.0, 0.0).astype(jnp.bfloat16)
    same = jnp.where(row_a == row_b, 1.0, 0.0).astype(jnp.bfloat16)
    pieces = jnp.zeros((LANES, ROWS), jnp.float32)
    for s in range(nsteps):
        names, scale = routes[s], weights[s]
        count = jnp.zeros((LANES, ROWS), jnp.float32)
        coef = jnp.zeros((LANES, ROWS), jnp.float32)
        for k in range(top):
            hit = names[k:k + 1] == expert
            count = count + jnp.where(hit, 1.0, 0.0)
            coef = coef + jnp.where(hit, scale[k:k + 1], 0.0)
        rank = jnp.dot(count.astype(jnp.bfloat16), before, preferred_element_type=jnp.float32)
        coef = jnp.where(rank < limit, coef, 0.0)
        first = coef.astype(jnp.bfloat16).astype(jnp.float32)
        second = (coef - first).astype(jnp.bfloat16).astype(jnp.float32)
        third = coef - first - second
        for n, value in enumerate((first, second, third)):
            pieces = jnp.where(piece == 3 * s + n, value, pieces)
    turned = lax.dot_general(
        same, pieces.astype(jnp.bfloat16), (((1,), (1,)), ((), ())), preferred_element_type=jnp.float32
    )
    rows_first[mine, pl.ds(width, LANES)] = turned.astype(jnp.bfloat16)

    pl.semaphore_wait(barrier, len(peers))

    sends = []

    def start(copy):
        copy.start()
        sends.append(copy)

    def gather_z(s, d):
        return remote(slot(s, me), slot(s, me), gz_send.at[s, d - 1], gz_recv.at[s, d - 1],
                      index(zs[d], x, c))

    def gather_x(s, d):
        ref = slot(s, index(zs[d], x, c))
        return remote(ref, ref, gx_send.at[s, d], gx_recv.at[s, d], partner_x)

    def gather_c(s, d, far):
        ref = slot(s, index(zs[d], (1 - x) if far else x, c))
        return remote(ref, ref, gc_send.at[s, d, far], gc_recv.at[s, d, far], partner_c)

    def wait_z(s, d):
        ref = slot(s, index(zs[d], x, c))
        remote(ref, ref, gz_send.at[s, d - 1], gz_recv.at[s, d - 1], index(zs[d], x, c)).wait_recv()

    def wait_x(s, d):
        ref = slot(s, index(zs[d], 1 - x, c))
        remote(ref, ref, gx_send.at[s, d], gx_recv.at[s, d], partner_x).wait_recv()

    def wait_c(s, d, far):
        ref = slot(s, index(zs[d], (1 - x) if far else x, 1 - c))
        remote(ref, ref, gc_send.at[s, d, far], gc_recv.at[s, d, far], partner_c).wait_recv()

    def gather_own(s):
        loads[s].wait()
        start(gather_x(s, 0))
        for d in (2, 3, 1):
            start(gather_z(s, d))
        start(gather_c(s, 0, 0))

    def gather_forward_z(s, d):
        wait_z(s, d)
        start(gather_x(s, d))
        start(gather_c(s, d, 0))

    def gather_forward_x(s, d):
        wait_x(s, d)
        start(gather_c(s, d, 1))

    def gather_end(s):
        for far in range(2):
            for d in range(4):
                wait_c(s, d, far)

    tile = 256

    def compute(s, first):
        if first:
            loads[nsteps].wait()
            loads[nsteps + 1].wait()
        for j in range(0, gate_w.shape[1], tile):
            inputs = rows[s][:, pl.ds(0, width)]
            gate = jnp.dot(inputs, gate_w[:, j:j + tile], preferred_element_type=jnp.float32)
            up = jnp.dot(inputs, up_w[:, j:j + tile], preferred_element_type=jnp.float32)
            hidden[:, j:j + tile] = (gate / (1.0 + jnp.exp(-gate)) * up).astype(jnp.bfloat16)
        if first:
            loads[nsteps + 2].wait()
        pick_row = lax.broadcasted_iota(jnp.int32, (LANES, tile), 0)
        pick = jnp.where((pick_row % experts == me) & (pick_row // (3 * experts) == s), 1.0, 0.0)
        coef = jnp.dot(
            rows_first[:, pl.ds(width, LANES)], pick.astype(jnp.bfloat16),
            preferred_element_type=jnp.float32,
        )
        for j in range(0, width, tile):
            result = jnp.dot(hidden[...], down_w[:, j:j + tile], preferred_element_type=jnp.float32)
            result = result.astype(jnp.bfloat16).astype(jnp.float32) * coef
            part[s, :, :, :, :, j:j + tile] = result.astype(jnp.bfloat16).reshape(4, 2, 2, ROWS, tile)

    def reduce_c(s):
        return remote(part.at[s, :, :, 1 - c], got_core.at[s], rc_send.at[s], rc_recv.at[s], partner_c)

    def reduce_x(s, d):
        return remote(sum_core.at[s, d], got_x.at[s, d], rx_send.at[s, d], rx_recv.at[s, d], partner_x)

    def reduce_z(s, d):
        return remote(sum_x.at[s, d - 1], got_z.at[s, d - 1], rz_send.at[s, d - 1], rz_recv.at[s, d - 1],
                      index(zs[d], x, c))

    def core_total(s, d, xx):
        return part[s, zs[d], xx, c].astype(jnp.float32) + got_core[s, zs[d], xx].astype(jnp.float32)

    def reduce_after_c(s):
        reduce_c(s).wait_recv()
        for d in (2, 3, 1, 0):
            sum_core[s, d] = core_total(s, d, 1 - x).astype(jnp.bfloat16)
            start(reduce_x(s, d))

    def x_total(s, d):
        reduce_x(s, d).wait_recv()
        return core_total(s, d, x) + got_x[s, d].astype(jnp.float32)

    def reduce_after_x(s):
        for d in (2, 3, 1):
            sum_x[s, d - 1] = x_total(s, d).astype(jnp.bfloat16)
            start(reduce_z(s, d))

    def reduce_end(s):
        total = x_total(s, 0)
        for d in (1, 2, 3):
            reduce_z(s, d).wait_recv()
            total = total + got_z[s, d - 1].astype(jnp.float32)
        out[s] = total.astype(jnp.bfloat16)

    gather_own(0)
    gather_own(1)
    gather_forward_z(0, 1)
    gather_forward_z(0, 2)
    gather_forward_z(0, 3)
    gather_forward_x(0, 0)
    gather_forward_z(1, 1)
    gather_forward_x(0, 1)
    gather_forward_x(0, 2)
    gather_forward_z(1, 2)
    gather_forward_x(0, 3)
    gather_forward_z(1, 3)
    gather_end(0)
    compute(0, True)
    start(reduce_c(0))
    for d in range(4):
        gather_forward_x(1, d)
    reduce_after_c(0)
    gather_end(1)
    compute(1, False)
    start(reduce_c(1))
    reduce_after_x(0)
    reduce_after_c(1)
    reduce_after_x(1)
    reduce_end(0)
    reduce_end(1)
    for copy in sends:
        copy.wait_send()


def fused(latent, routes, combine_weights, keep, w_gate, w_up, w_down):
    nsteps, nrows, width = latent.shape
    units = w_gate.shape[2]
    blocks = 16 * nrows
    bf16 = jnp.bfloat16
    dma = pltpu.SemaphoreType.DMA
    vmem = pl.BlockSpec(memory_space=pltpu.VMEM)
    hbm = pl.BlockSpec(memory_space=pltpu.HBM)
    return pl.pallas_call(
        fused_kernel,
        out_shape=jax.ShapeDtypeStruct(latent.shape, bf16),
        in_specs=[hbm, vmem, vmem, pl.BlockSpec(memory_space=pltpu.SMEM), hbm, hbm, hbm],
        out_specs=vmem,
        scratch_shapes=[
            pltpu.VMEM((blocks, width + LANES), bf16),
            pltpu.VMEM((nsteps - 1, blocks, width), bf16),
            pltpu.VMEM((width, units), bf16),
            pltpu.VMEM((width, units), bf16),
            pltpu.VMEM((units, width), bf16),
            pltpu.VMEM((blocks, units), bf16),
            pltpu.VMEM((nsteps, 4, 2, 2, nrows, width), bf16),
            pltpu.VMEM((nsteps, 4, 2, nrows, width), bf16),
            pltpu.VMEM((nsteps, 4, nrows, width), bf16),
            pltpu.VMEM((nsteps, 4, nrows, width), bf16),
            pltpu.VMEM((nsteps, 3, nrows, width), bf16),
            pltpu.VMEM((nsteps, 3, nrows, width), bf16),
            dma((nsteps + 3,)),
            dma((nsteps, 3)), dma((nsteps, 3)),
            dma((nsteps, 4)), dma((nsteps, 4)),
            dma((nsteps, 4, 2)), dma((nsteps, 4, 2)),
            dma((nsteps,)), dma((nsteps,)),
            dma((nsteps, 4)), dma((nsteps, 4)),
            dma((nsteps, 3)), dma((nsteps, 3)),
        ],
        compiler_params=pltpu.CompilerParams(
            collective_id=0, has_side_effects=True, vmem_limit_bytes=60 * 1024 * 1024
        ),
        cost_estimate=pl.CostEstimate(
            flops=6 * nsteps * blocks * width * units,
            bytes_accessed=6 * width * units,
            transcendentals=nsteps * blocks * units,
        ),
    )(latent, jnp.swapaxes(routes, 1, 2), jnp.swapaxes(combine_weights, 1, 2), keep, w_gate, w_up, w_down)


def solution(mesh):
    one_group = mesh.shape["ep"] == 16 and mesh.shape["tp"] == 1
    placed = (
        P(None, ("groups", "ep"), "tp"),
        P(None, ("groups", "ep"), None),
        P(None, ("groups", "ep"), None),
        P(),
        P("ep", None, "tp"),
        P("ep", None, "tp"),
        P("ep", "tp", None),
    )
    return jax.shard_map(
        fused if one_group else shards,
        mesh=mesh,
        in_specs=placed,
        out_specs=P(None, ("groups", "ep"), "tp"),
        check_vma=False,
    )
```

```python
import jax
import jax.numpy as jnp
from jax import lax
from jax.experimental import pallas as pl
from jax.experimental.pallas import tpu as pltpu
from jax.sharding import PartitionSpec as P

ROWS = 16
LANES = 128
MESH = pl.DeviceIdType.MESH


def shards(latent, routes, combine_weights, keep, w_gate, w_up, w_down):
    nsteps, rows_dev, top = routes.shape
    experts = keep.shape[0]
    capacity = min(rows_dev, max(2, 3 * rows_dev * top // (2 * experts)))
    onehot = (routes[..., None] == jnp.arange(experts, dtype=jnp.int32)).astype(jnp.int32)
    per_row = jnp.sum(onehot, axis=2)
    before = jnp.cumsum(per_row, axis=1) - per_row
    rank = jnp.take_along_axis(before, routes, axis=2)
    limits = jnp.sum(onehot * keep, axis=3)
    kept = rank < limits
    dropped = experts * capacity
    slot_index = jnp.where(kept, routes * capacity + rank, dropped)
    source = lax.all_gather(latent, "tp", axis=2, tiled=True)
    send_width = source.shape[2]

    def pack(rows_step, slots_step):
        spread = jnp.broadcast_to(rows_step[:, None, :], (rows_dev, top, send_width)).reshape(
            rows_dev * top, send_width
        )
        buffer = (
            jnp.zeros((dropped + 1, send_width), rows_step.dtype)
            .at[slots_step.reshape(-1)]
            .set(spread)
        )
        return buffer[:dropped].reshape(experts, capacity, send_width)

    def serve(received):
        gate = jnp.einsum("sil,lh->sih", received, w_gate[0], preferred_element_type=jnp.float32)
        up = jnp.einsum("sil,lh->sih", received, w_up[0], preferred_element_type=jnp.float32)
        hidden = (jax.nn.silu(gate) * up).astype(jnp.bfloat16)
        partial_out = jnp.einsum(
            "sih,hl->sil", hidden, w_down[0], preferred_element_type=jnp.float32
        )
        summed = lax.psum_scatter(
            partial_out.astype(jnp.bfloat16), "tp", scatter_dimension=2, tiled=True
        )
        return lax.all_to_all(summed, "ep", split_axis=0, concat_axis=0, tiled=True)

    def deliver(buffer):
        return serve(lax.all_to_all(buffer, "ep", split_axis=0, concat_axis=0, tiled=True))

    buffers = [pack(source[step], slot_index[step]) for step in range(nsteps)]
    returned = [deliver(buffer) for buffer in buffers]
    outputs = []
    for step in range(nsteps):
        back = returned[step]
        half_width = back.shape[2]
        flat_back = jnp.concatenate(
            [back.reshape(dropped, half_width), jnp.zeros((1, half_width), back.dtype)], axis=0
        )
        picked = flat_back[slot_index[step]]
        total = jnp.sum(picked.astype(jnp.float32) * combine_weights[step][..., None], axis=1)
        outputs.append(total.astype(jnp.bfloat16))
    return jnp.stack(outputs, axis=0)


def fused_kernel(
    latent, routes_in, weights_in, keep_in, w_gate, w_up, w_down, out,
    rows_first, rows_next, gate_w, up_w, down_w, hidden, part, got_core, sum_core, got_x, sum_x, got_z,
    routes, weights, keep, load_sem, small_sem, gz_send, gz_recv, gx_send, gx_recv, gc_send, gc_recv,
    rc_send, rc_recv, rx_send, rx_recv, rz_send, rz_recv,
):
    nsteps, top, _ = routes.shape
    width = latent.shape[2]
    me = lax.axis_index("ep")
    z, x, c = me // 4, (me // 2) % 2, me % 2
    zs = (z, z + 1 - 2 * (z % 2), (z + 2) % 4, 3 - z)

    def index(zz, xx, cc):
        return zz * 4 + xx * 2 + cc

    rows = (rows_first, *(rows_next.at[s] for s in range(nsteps - 1)))

    def slot(s, owner):
        return rows[s].at[pl.ds(pl.multiple_of(owner * ROWS, ROWS), ROWS)]

    def remote(src, dst, send, recv, device):
        return pltpu.make_async_remote_copy(
            src_ref=src, dst_ref=dst, send_sem=send, recv_sem=recv,
            device_id={"ep": device}, device_id_type=MESH,
        )

    partner_x, partner_c = index(z, 1 - x, c), index(z, x, 1 - c)
    barrier = pltpu.get_barrier_semaphore()
    peers = [index(zs[1], x, c), index(zs[2], x, c), index(zs[3], x, c), partner_x, partner_c]
    for peer in peers:
        pl.semaphore_signal(barrier, inc=1, device_id={"ep": peer}, device_id_type=MESH)

    mine = pl.ds(pl.multiple_of(me * ROWS, ROWS), ROWS)
    loads = [
        pltpu.make_async_copy(latent.at[s], rows[s].at[mine, pl.ds(0, width)], load_sem.at[s])
        for s in range(nsteps)
    ]
    for n, (src, dst) in enumerate(((w_gate, gate_w), (w_up, up_w), (w_down, down_w))):
        loads.append(pltpu.make_async_copy(src.at[0], dst, load_sem.at[nsteps + n]))
    smalls = [
        pltpu.make_async_copy(src, dst, small_sem.at[n])
        for n, (src, dst) in enumerate(((routes_in, routes), (weights_in, weights), (keep_in, keep)))
    ]
    for load in smalls + loads:
        load.start()
    for load in smalls:
        load.wait()

    experts = keep.shape[0]
    line = lax.broadcasted_iota(jnp.int32, (LANES, ROWS), 0)
    expert = line % experts
    piece = line // experts
    limit = jnp.zeros((LANES, ROWS), jnp.float32)
    for e in range(experts):
        limit = jnp.where(expert == e, keep[e].astype(jnp.float32), limit)
    row_a = lax.broadcasted_iota(jnp.int32, (ROWS, ROWS), 0)
    row_b = lax.broadcasted_iota(jnp.int32, (ROWS, ROWS), 1)
    before = jnp.where(row_a < row_b, 1.0, 0.0).astype(jnp.bfloat16)
    same = jnp.where(row_a == row_b, 1.0, 0.0).astype(jnp.bfloat16)
    pieces = jnp.zeros((LANES, ROWS), jnp.float32)
    for s in range(nsteps):
        names, scale = routes[s], weights[s]
        count = jnp.zeros((LANES, ROWS), jnp.float32)
        coef = jnp.zeros((LANES, ROWS), jnp.float32)
        for k in range(top):
            hit = names[k:k + 1] == expert
            count = count + jnp.where(hit, 1.0, 0.0)
            coef = coef + jnp.where(hit, scale[k:k + 1], 0.0)
        rank = jnp.dot(count.astype(jnp.bfloat16), before, preferred_element_type=jnp.float32)
        coef = jnp.where(rank < limit, coef, 0.0)
        first = coef.astype(jnp.bfloat16).astype(jnp.float32)
        second = (coef - first).astype(jnp.bfloat16).astype(jnp.float32)
        third = coef - first - second
        for n, value in enumerate((first, second, third)):
            pieces = jnp.where(piece == 3 * s + n, value, pieces)
    turned = lax.dot_general(
        same, pieces.astype(jnp.bfloat16), (((1,), (1,)), ((), ())), preferred_element_type=jnp.float32
    )
    rows_first[mine, pl.ds(width, LANES)] = turned.astype(jnp.bfloat16)

    pl.semaphore_wait(barrier, len(peers))

    sends = []

    def start(copy):
        copy.start()
        sends.append(copy)

    def gather_z(s, d):
        owner, to = me, d
        return remote(slot(s, owner), slot(s, owner), gz_send.at[s, d - 1], gz_recv.at[s, d - 1],
                      index(zs[to], x, c))

    def gather_x(s, d):
        ref = slot(s, index(zs[d], x, c))
        return remote(ref, ref, gx_send.at[s, d], gx_recv.at[s, d], partner_x)

    def gather_c(s, d, far):
        ref = slot(s, index(zs[d], (1 - x) if far else x, c))
        return remote(ref, ref, gc_send.at[s, d, far], gc_recv.at[s, d, far], partner_c)

    def wait_z(s, d):
        ref = slot(s, index(zs[d], x, c))
        remote(ref, ref, gz_send.at[s, d - 1], gz_recv.at[s, d - 1], index(zs[1], x, c)).wait_recv()

    def wait_x(s, d):
        ref = slot(s, index(zs[d], 1 - x, c))
        remote(ref, ref, gx_send.at[s, d], gx_recv.at[s, d], partner_x).wait_recv()

    def wait_c(s, d, far):
        ref = slot(s, index(zs[d], (1 - x) if far else x, 1 - c))
        remote(ref, ref, gc_send.at[s, d, far], gc_recv.at[s, d, far], partner_c).wait_recv()

    def gather_own(s):
        loads[s].wait()
        start(gather_x(s, 0))
        for d in (2, 3, 1):
            start(gather_z(s, d))
        start(gather_c(s, 0, 0))

    def gather_forward_z(s, d):
        wait_z(s, d)
        start(gather_x(s, d))
        start(gather_c(s, d, 0))

    def gather_forward_x(s, d):
        wait_x(s, d)
        start(gather_c(s, d, 1))

    def pair_of(h):
        return z // 2 if h == 0 else 1 - z // 2

    def gather_end(s, h):
        for far in range(2):
            for d in (2 * h, 2 * h + 1):
                wait_c(s, d, far)

    tile = 256

    half = rows_first.shape[0] // 2

    def compute(s, h, first=False):
        pair = pair_of(h)
        held = pl.ds(pl.multiple_of(pair * half, half), half)
        if first:
            loads[nsteps].wait()
            loads[nsteps + 1].wait()
        for j in range(0, gate_w.shape[1], tile):
            inputs = rows[s][held, pl.ds(0, width)]
            gate = jnp.dot(inputs, gate_w[:, j:j + tile], preferred_element_type=jnp.float32)
            up = jnp.dot(inputs, up_w[:, j:j + tile], preferred_element_type=jnp.float32)
            hidden[:, j:j + tile] = (gate / (1.0 + jnp.exp(-gate)) * up).astype(jnp.bfloat16)
        if first:
            loads[nsteps + 2].wait()
        pick_row = lax.broadcasted_iota(jnp.int32, (LANES, tile), 0)
        pick = jnp.where((pick_row % experts == me) & (pick_row // (3 * experts) == s), 1.0, 0.0)
        coef = jnp.dot(
            rows_first[held, pl.ds(width, LANES)], pick.astype(jnp.bfloat16),
            preferred_element_type=jnp.float32,
        )
        for j in range(0, width, tile):
            result = jnp.dot(hidden[...], down_w[:, j:j + tile], preferred_element_type=jnp.float32)
            result = result.astype(jnp.bfloat16).astype(jnp.float32) * coef
            part[s, pl.ds(2 * pair, 2), :, :, :, j:j + tile] = (
                result.astype(jnp.bfloat16).reshape(2, 2, 2, ROWS, tile)
            )

    def reduce_c(s, h):
        held = pl.ds(2 * pair_of(h), 2)
        return remote(part.at[s, held, :, 1 - c], got_core.at[s, held], rc_send.at[s, h],
                      rc_recv.at[s, h], partner_c)

    def compute_send(s, h, first=False):
        gather_end(s, h)
        compute(s, h, first)
        start(reduce_c(s, h))

    def reduce_x(s, d):
        return remote(sum_core.at[s, d], got_x.at[s, d], rx_send.at[s, d], rx_recv.at[s, d], partner_x)

    def reduce_z(s, d):
        return remote(sum_x.at[s, d - 1], got_z.at[s, d - 1], rz_send.at[s, d - 1], rz_recv.at[s, d - 1],
                      index(zs[d], x, c))

    def core_total(s, d, xx):
        return part[s, zs[d], xx, c].astype(jnp.float32) + got_core[s, zs[d], xx].astype(jnp.float32)

    def reduce_after_c(s, h):
        reduce_c(s, h).wait_recv()
        for d in ((1, 0), (2, 3))[h]:
            sum_core[s, d] = core_total(s, d, 1 - x).astype(jnp.bfloat16)
            start(reduce_x(s, d))

    def x_total(s, d):
        reduce_x(s, d).wait_recv()
        return core_total(s, d, x) + got_x[s, d].astype(jnp.float32)

    def reduce_after_x(s, h):
        for d in ((1,), (2, 3))[h]:
            sum_x[s, d - 1] = x_total(s, d).astype(jnp.bfloat16)
            start(reduce_z(s, d))

    def reduce_end(s):
        total = x_total(s, 0)
        for d in (1, 2, 3):
            reduce_z(s, d).wait_recv()
            total = total + got_z[s, d - 1].astype(jnp.float32)
        out[s] = total.astype(jnp.bfloat16)

    gather_own(0)
    gather_own(1)
    gather_forward_z(0, 1)
    gather_forward_z(0, 2)
    gather_forward_z(0, 3)
    gather_forward_x(0, 0)
    gather_forward_z(1, 1)
    gather_forward_x(0, 1)
    gather_forward_x(0, 2)
    gather_forward_z(1, 2)
    gather_forward_x(0, 3)
    gather_forward_z(1, 3)
    compute_send(0, 0, True)
    compute_send(0, 1)
    gather_forward_x(1, 0)
    gather_forward_x(1, 1)
    gather_forward_x(1, 2)
    gather_forward_x(1, 3)
    reduce_after_c(0, 1)
    reduce_after_c(0, 0)
    compute_send(1, 0)
    compute_send(1, 1)
    reduce_after_x(0, 1)
    reduce_after_c(1, 1)
    reduce_after_c(1, 0)
    reduce_after_x(0, 0)
    reduce_after_x(1, 1)
    reduce_end(0)
    reduce_after_x(1, 0)
    reduce_end(1)
    for copy in sends:
        copy.wait_send()


def fused(latent, routes, combine_weights, keep, w_gate, w_up, w_down):
    nsteps, nrows, width = latent.shape
    units = w_gate.shape[2]
    blocks = 16 * nrows
    bf16 = jnp.bfloat16
    dma = pltpu.SemaphoreType.DMA
    vmem = pl.BlockSpec(memory_space=pltpu.VMEM)
    hbm = pl.BlockSpec(memory_space=pltpu.HBM)
    return pl.pallas_call(
        fused_kernel,
        out_shape=jax.ShapeDtypeStruct(latent.shape, bf16),
        in_specs=[hbm] * 7,
        out_specs=vmem,
        scratch_shapes=[
            pltpu.VMEM((blocks, width + LANES), bf16),
            pltpu.VMEM((nsteps - 1, blocks, width), bf16),
            pltpu.VMEM((width, units), bf16),
            pltpu.VMEM((width, units), bf16),
            pltpu.VMEM((units, width), bf16),
            pltpu.VMEM((blocks // 2, units), bf16),
            pltpu.VMEM((nsteps, 4, 2, 2, nrows, width), bf16),
            pltpu.VMEM((nsteps, 4, 2, nrows, width), bf16),
            pltpu.VMEM((nsteps, 4, nrows, width), bf16),
            pltpu.VMEM((nsteps, 4, nrows, width), bf16),
            pltpu.VMEM((nsteps, 3, nrows, width), bf16),
            pltpu.VMEM((nsteps, 3, nrows, width), bf16),
            pltpu.VMEM((nsteps, routes.shape[2], nrows), jnp.int32),
            pltpu.VMEM((nsteps, routes.shape[2], nrows), jnp.float32),
            pltpu.SMEM(keep.shape, jnp.int32),
            dma((nsteps + 3,)), dma((3,)),
            dma((nsteps, 3)), dma((nsteps, 3)),
            dma((nsteps, 4)), dma((nsteps, 4)),
            dma((nsteps, 4, 2)), dma((nsteps, 4, 2)),
            dma((nsteps, 2)), dma((nsteps, 2)),
            dma((nsteps, 4)), dma((nsteps, 4)),
            dma((nsteps, 3)), dma((nsteps, 3)),
        ],
        compiler_params=pltpu.CompilerParams(
            collective_id=0, has_side_effects=True, vmem_limit_bytes=60 * 1024 * 1024
        ),
        cost_estimate=pl.CostEstimate(
            flops=6 * nsteps * blocks * width * units,
            bytes_accessed=6 * width * units,
            transcendentals=nsteps * blocks * units,
        ),
    )(latent, jnp.swapaxes(routes, 1, 2), jnp.swapaxes(combine_weights, 1, 2), keep, w_gate, w_up, w_down)


def solution(mesh):
    one_group = mesh.shape["ep"] == 16 and mesh.shape["tp"] == 1
    placed = (
        P(None, ("groups", "ep"), "tp"),
        P(None, ("groups", "ep"), None),
        P(None, ("groups", "ep"), None),
        P(),
        P("ep", None, "tp"),
        P("ep", None, "tp"),
        P("ep", "tp", None),
    )
    return jax.shard_map(
        fused if one_group else shards,
        mesh=mesh,
        in_specs=placed,
        out_specs=P(None, ("groups", "ep"), "tp"),
        check_vma=False,
    )
```

```python
import jax
import jax.numpy as jnp
from jax import lax
from jax.experimental import pallas as pl
from jax.experimental.pallas import tpu as pltpu
from jax.sharding import PartitionSpec as P

ROWS = 16
LANES = 128
MESH = pl.DeviceIdType.MESH


def shards(latent, routes, combine_weights, keep, w_gate, w_up, w_down):
    nsteps, rows_dev, top = routes.shape
    experts = keep.shape[0]
    capacity = min(rows_dev, max(2, 3 * rows_dev * top // (2 * experts)))
    onehot = (routes[..., None] == jnp.arange(experts, dtype=jnp.int32)).astype(jnp.int32)
    per_row = jnp.sum(onehot, axis=2)
    before = jnp.cumsum(per_row, axis=1) - per_row
    rank = jnp.take_along_axis(before, routes, axis=2)
    limits = jnp.sum(onehot * keep, axis=3)
    kept = rank < limits
    dropped = experts * capacity
    slot_index = jnp.where(kept, routes * capacity + rank, dropped)
    source = lax.all_gather(latent, "tp", axis=2, tiled=True)
    send_width = source.shape[2]

    def pack(rows_step, slots_step):
        spread = jnp.broadcast_to(rows_step[:, None, :], (rows_dev, top, send_width)).reshape(
            rows_dev * top, send_width
        )
        buffer = (
            jnp.zeros((dropped + 1, send_width), rows_step.dtype)
            .at[slots_step.reshape(-1)]
            .set(spread)
        )
        return buffer[:dropped].reshape(experts, capacity, send_width)

    def serve(received):
        gate = jnp.einsum("sil,lh->sih", received, w_gate[0], preferred_element_type=jnp.float32)
        up = jnp.einsum("sil,lh->sih", received, w_up[0], preferred_element_type=jnp.float32)
        hidden = (jax.nn.silu(gate) * up).astype(jnp.bfloat16)
        partial_out = jnp.einsum(
            "sih,hl->sil", hidden, w_down[0], preferred_element_type=jnp.float32
        )
        summed = lax.psum_scatter(
            partial_out.astype(jnp.bfloat16), "tp", scatter_dimension=2, tiled=True
        )
        return lax.all_to_all(summed, "ep", split_axis=0, concat_axis=0, tiled=True)

    def deliver(buffer):
        return serve(lax.all_to_all(buffer, "ep", split_axis=0, concat_axis=0, tiled=True))

    buffers = [pack(source[step], slot_index[step]) for step in range(nsteps)]
    returned = [deliver(buffer) for buffer in buffers]
    outputs = []
    for step in range(nsteps):
        back = returned[step]
        half_width = back.shape[2]
        flat_back = jnp.concatenate(
            [back.reshape(dropped, half_width), jnp.zeros((1, half_width), back.dtype)], axis=0
        )
        picked = flat_back[slot_index[step]]
        total = jnp.sum(picked.astype(jnp.float32) * combine_weights[step][..., None], axis=1)
        outputs.append(total.astype(jnp.bfloat16))
    return jnp.stack(outputs, axis=0)


def fused_kernel(
    latent, routes_in, weights_in, keep_in, w_gate, w_up, w_down, out_hbm,
    rows_first, rows_next, gate_w, up_w, down_w, hidden, part, got_core, sum_core, got_x, sum_x, got_z,
    out, routes, weights, keep, load_sem, small_sem, out_sem, gz_send, gz_recv, gx_send, gx_recv, gc_send, gc_recv,
    rc_send, rc_recv, rx_send, rx_recv, rz_send, rz_recv,
):
    nsteps, top, _ = routes.shape
    width = latent.shape[2]
    me = lax.axis_index("ep")
    z, x, c = me // 4, (me // 2) % 2, me % 2
    zs = (z, z + 1 - 2 * (z % 2), (z + 2) % 4, 3 - z)

    def index(zz, xx, cc):
        return zz * 4 + xx * 2 + cc

    rows = (rows_first, *(rows_next.at[s] for s in range(nsteps - 1)))

    def slot(s, owner):
        return rows[s].at[pl.ds(pl.multiple_of(owner * ROWS, ROWS), ROWS)]

    def remote(src, dst, send, recv, device):
        return pltpu.make_async_remote_copy(
            src_ref=src, dst_ref=dst, send_sem=send, recv_sem=recv,
            device_id={"ep": device}, device_id_type=MESH,
        )

    partner_x, partner_c = index(z, 1 - x, c), index(z, x, 1 - c)
    barrier = pltpu.get_barrier_semaphore()
    peers = [index(zs[1], x, c), index(zs[2], x, c), partner_x, partner_c]
    for peer in peers:
        pl.semaphore_signal(barrier, inc=1, device_id={"ep": peer}, device_id_type=MESH)

    mine = pl.ds(pl.multiple_of(me * ROWS, ROWS), ROWS)
    loads = [
        pltpu.make_async_copy(latent.at[s], rows[s].at[mine, pl.ds(0, width)], load_sem.at[s])
        for s in range(nsteps)
    ]
    for n, (src, dst) in enumerate(((w_gate, gate_w), (w_up, up_w), (w_down, down_w))):
        loads.append(pltpu.make_async_copy(src.at[0], dst, load_sem.at[nsteps + n]))
    smalls = [
        pltpu.make_async_copy(src, dst, small_sem.at[n])
        for n, (src, dst) in enumerate(((routes_in, routes), (weights_in, weights), (keep_in, keep)))
    ]
    for load in smalls + loads:
        load.start()
    for load in smalls:
        load.wait()

    experts = keep.shape[0]
    line = lax.broadcasted_iota(jnp.int32, (LANES, ROWS), 0)
    expert = line % experts
    piece = line // experts
    limit = jnp.zeros((LANES, ROWS), jnp.float32)
    for e in range(experts):
        limit = jnp.where(expert == e, keep[e].astype(jnp.float32), limit)
    row_a = lax.broadcasted_iota(jnp.int32, (ROWS, ROWS), 0)
    row_b = lax.broadcasted_iota(jnp.int32, (ROWS, ROWS), 1)
    before = jnp.where(row_a < row_b, 1.0, 0.0).astype(jnp.bfloat16)
    same = jnp.where(row_a == row_b, 1.0, 0.0).astype(jnp.bfloat16)
    pieces = jnp.zeros((LANES, ROWS), jnp.float32)
    for s in range(nsteps):
        names, scale = routes[s], weights[s]
        count = jnp.zeros((LANES, ROWS), jnp.float32)
        coef = jnp.zeros((LANES, ROWS), jnp.float32)
        for k in range(top):
            hit = names[k:k + 1] == expert
            count = count + jnp.where(hit, 1.0, 0.0)
            coef = coef + jnp.where(hit, scale[k:k + 1], 0.0)
        rank = jnp.dot(count.astype(jnp.bfloat16), before, preferred_element_type=jnp.float32)
        coef = jnp.where(rank < limit, coef, 0.0)
        first = coef.astype(jnp.bfloat16).astype(jnp.float32)
        second = (coef - first).astype(jnp.bfloat16).astype(jnp.float32)
        third = coef - first - second
        for n, value in enumerate((first, second, third)):
            pieces = jnp.where(piece == 3 * s + n, value, pieces)
    turned = lax.dot_general(
        same, pieces.astype(jnp.bfloat16), (((1,), (1,)), ((), ())), preferred_element_type=jnp.float32
    )
    rows_first[mine, pl.ds(width, LANES)] = turned.astype(jnp.bfloat16)

    pl.semaphore_wait(barrier, len(peers))

    sends = []
    stores = []

    def start(copy):
        copy.start()
        sends.append(copy)

    def gather_z(s, d):
        owner, to = (me, d) if d < 3 else (index(zs[2], x, c), 1)
        return remote(slot(s, owner), slot(s, owner), gz_send.at[s, d - 1], gz_recv.at[s, d - 1],
                      index(zs[to], x, c))

    def gather_x(s, d):
        ref = slot(s, index(zs[d], x, c))
        return remote(ref, ref, gx_send.at[s, d], gx_recv.at[s, d], partner_x)

    def gather_c(s, d, far):
        ref = slot(s, index(zs[d], (1 - x) if far else x, c))
        return remote(ref, ref, gc_send.at[s, d, far], gc_recv.at[s, d, far], partner_c)

    def wait_z(s, d):
        ref = slot(s, index(zs[d], x, c))
        remote(ref, ref, gz_send.at[s, d - 1], gz_recv.at[s, d - 1], index(zs[1], x, c)).wait_recv()

    def wait_x(s, d):
        ref = slot(s, index(zs[d], 1 - x, c))
        remote(ref, ref, gx_send.at[s, d], gx_recv.at[s, d], partner_x).wait_recv()

    def wait_c(s, d, far):
        ref = slot(s, index(zs[d], (1 - x) if far else x, 1 - c))
        remote(ref, ref, gc_send.at[s, d, far], gc_recv.at[s, d, far], partner_c).wait_recv()

    def gather_own(s):
        loads[s].wait()
        start(gather_x(s, 0))
        start(gather_z(s, 2))
        start(gather_z(s, 1))
        start(gather_c(s, 0, 0))

    def gather_forward_z(s, d):
        wait_z(s, d)
        if d == 2:
            start(gather_z(s, 3))
        start(gather_x(s, d))
        start(gather_c(s, d, 0))

    def gather_forward_x(s, d):
        wait_x(s, d)
        start(gather_c(s, d, 1))

    def pair_of(h):
        return z // 2 if h == 0 else 1 - z // 2

    def gather_end(s, h):
        for far in range(2):
            for d in (2 * h, 2 * h + 1):
                wait_c(s, d, far)

    tile = 256

    half = rows_first.shape[0] // 2

    def compute(s, h, first=False):
        pair = pair_of(h)
        held = pl.ds(pl.multiple_of(pair * half, half), half)
        if first:
            loads[nsteps].wait()
            loads[nsteps + 1].wait()
        for j in range(0, gate_w.shape[1], tile):
            inputs = rows[s][held, pl.ds(0, width)]
            gate = jnp.dot(inputs, gate_w[:, j:j + tile], preferred_element_type=jnp.float32)
            up = jnp.dot(inputs, up_w[:, j:j + tile], preferred_element_type=jnp.float32)
            hidden[:, j:j + tile] = (gate / (1.0 + jnp.exp(-gate)) * up).astype(jnp.bfloat16)
        if first:
            loads[nsteps + 2].wait()
        pick_row = lax.broadcasted_iota(jnp.int32, (LANES, tile), 0)
        pick = jnp.where((pick_row % experts == me) & (pick_row // (3 * experts) == s), 1.0, 0.0)
        coef = jnp.dot(
            rows_first[held, pl.ds(width, LANES)], pick.astype(jnp.bfloat16),
            preferred_element_type=jnp.float32,
        )
        for j in range(0, width, tile):
            result = jnp.dot(hidden[...], down_w[:, j:j + tile], preferred_element_type=jnp.float32)
            result = result.astype(jnp.bfloat16).astype(jnp.float32) * coef
            part[s, pl.ds(2 * pair, 2), :, :, :, j:j + tile] = (
                result.astype(jnp.bfloat16).reshape(2, 2, 2, ROWS, tile)
            )

    def reduce_c(s, h):
        held = pl.ds(2 * pair_of(h), 2)
        return remote(part.at[s, held, :, 1 - c], got_core.at[s, held], rc_send.at[s, h],
                      rc_recv.at[s, h], partner_c)

    def compute_send(s, h, first=False):
        gather_end(s, h)
        compute(s, h, first)
        start(reduce_c(s, h))

    def reduce_x(s, d):
        return remote(sum_core.at[s, d], got_x.at[s, d], rx_send.at[s, d], rx_recv.at[s, d], partner_x)

    def reduce_z(s, d):
        return remote(sum_x.at[s, d - 1], got_z.at[s, d - 1], rz_send.at[s, d - 1], rz_recv.at[s, d - 1],
                      index(zs[d], x, c))

    def core_total(s, d, xx):
        return part[s, zs[d], xx, c].astype(jnp.float32) + got_core[s, zs[d], xx].astype(jnp.float32)

    def reduce_after_c(s, h):
        reduce_c(s, h).wait_recv()
        for d in ((1, 0), (2, 3))[h]:
            sum_core[s, d] = core_total(s, d, 1 - x).astype(jnp.bfloat16)
            start(reduce_x(s, d))

    def x_total(s, d):
        reduce_x(s, d).wait_recv()
        return core_total(s, d, x) + got_x[s, d].astype(jnp.float32)

    def reduce_after_x(s, h):
        for d in ((1,), (2, 3))[h]:
            sum_x[s, d - 1] = x_total(s, d).astype(jnp.bfloat16)
            start(reduce_z(s, d))

    def reduce_end(s):
        total = x_total(s, 0)
        for d in (1, 2, 3):
            reduce_z(s, d).wait_recv()
            total = total + got_z[s, d - 1].astype(jnp.float32)
        out[s] = total.astype(jnp.bfloat16)
        copy = pltpu.make_async_copy(out.at[s], out_hbm.at[s], out_sem.at[s])
        copy.start()
        stores.append(copy)

    gather_own(0)
    gather_own(1)
    gather_forward_z(0, 2)
    gather_forward_z(0, 1)
    gather_forward_z(1, 2)
    gather_forward_z(1, 1)
    gather_forward_x(0, 0)
    gather_forward_z(0, 3)
    gather_forward_x(0, 2)
    gather_forward_x(0, 1)
    gather_forward_z(1, 3)
    gather_forward_x(0, 3)
    compute_send(0, 0, True)
    gather_forward_x(1, 0)
    gather_forward_x(1, 2)
    gather_forward_x(1, 1)
    compute_send(0, 1)
    gather_forward_x(1, 3)
    reduce_after_c(0, 1)
    reduce_after_c(0, 0)
    compute_send(1, 0)
    compute_send(1, 1)
    reduce_after_x(0, 1)
    reduce_after_c(1, 1)
    reduce_after_c(1, 0)
    reduce_after_x(0, 0)
    reduce_after_x(1, 1)
    reduce_end(0)
    reduce_after_x(1, 0)
    reduce_end(1)
    for copy in sends:
        copy.wait_send()
    for copy in stores:
        copy.wait()


def fused(latent, routes, combine_weights, keep, w_gate, w_up, w_down):
    nsteps, nrows, width = latent.shape
    units = w_gate.shape[2]
    blocks = 16 * nrows
    bf16 = jnp.bfloat16
    dma = pltpu.SemaphoreType.DMA
    hbm = pl.BlockSpec(memory_space=pltpu.HBM)
    return pl.pallas_call(
        fused_kernel,
        out_shape=jax.ShapeDtypeStruct(latent.shape, bf16),
        in_specs=[hbm] * 7,
        out_specs=hbm,
        scratch_shapes=[
            pltpu.VMEM((blocks, width + LANES), bf16),
            pltpu.VMEM((nsteps - 1, blocks, width), bf16),
            pltpu.VMEM((width, units), bf16),
            pltpu.VMEM((width, units), bf16),
            pltpu.VMEM((units, width), bf16),
            pltpu.VMEM((blocks // 2, units), bf16),
            pltpu.VMEM((nsteps, 4, 2, 2, nrows, width), bf16),
            pltpu.VMEM((nsteps, 4, 2, nrows, width), bf16),
            pltpu.VMEM((nsteps, 4, nrows, width), bf16),
            pltpu.VMEM((nsteps, 4, nrows, width), bf16),
            pltpu.VMEM((nsteps, 3, nrows, width), bf16),
            pltpu.VMEM((nsteps, 3, nrows, width), bf16),
            pltpu.VMEM(latent.shape, bf16),
            pltpu.VMEM((nsteps, routes.shape[2], nrows), jnp.int32),
            pltpu.VMEM((nsteps, routes.shape[2], nrows), jnp.float32),
            pltpu.SMEM(keep.shape, jnp.int32),
            dma((nsteps + 3,)), dma((3,)), dma((nsteps,)),
            dma((nsteps, 3)), dma((nsteps, 3)),
            dma((nsteps, 4)), dma((nsteps, 4)),
            dma((nsteps, 4, 2)), dma((nsteps, 4, 2)),
            dma((nsteps, 2)), dma((nsteps, 2)),
            dma((nsteps, 4)), dma((nsteps, 4)),
            dma((nsteps, 3)), dma((nsteps, 3)),
        ],
        compiler_params=pltpu.CompilerParams(
            collective_id=0, has_side_effects=True, vmem_limit_bytes=60 * 1024 * 1024
        ),
        cost_estimate=pl.CostEstimate(
            flops=6 * nsteps * blocks * width * units,
            bytes_accessed=6 * width * units,
            transcendentals=nsteps * blocks * units,
        ),
    )(latent, jnp.swapaxes(routes, 1, 2), jnp.swapaxes(combine_weights, 1, 2), keep, w_gate, w_up, w_down)


def solution(mesh):
    one_group = mesh.shape["ep"] == 16 and mesh.shape["tp"] == 1
    placed = (
        P(None, ("groups", "ep"), "tp"),
        P(None, ("groups", "ep"), None),
        P(None, ("groups", "ep"), None),
        P(),
        P("ep", None, "tp"),
        P("ep", None, "tp"),
        P("ep", "tp", None),
    )
    return jax.shard_map(
        fused if one_group else shards,
        mesh=mesh,
        in_specs=placed,
        out_specs=P(None, ("groups", "ep"), "tp"),
        check_vma=False,
    )
```
